32 devices in a mesh: groups: 2 (over x), seg: 8 (over z, y), head: 2 (over core).
Axes of the slice: x: 2, y: 2, z: 4, core: 2. Of those that a mesh axis runs over, the one named last changes fastest.
Arguments:
- features: bfloat16 [32768, 128], P(('groups', 'seg', 'head')), parts along dimension 0, may hold values from -6 to 6
- positions: int32 [32768], P(('groups', 'seg', 'head')), parts along dimension 0, may hold values from 0 to 16383, as said below
- neighbors: int32 [32768, 27], P(('groups', 'seg', 'head')), parts along dimension 0, may hold values from -1 to 1535, as said below
- send_rows: int32 [128, 128], P(('groups', 'seg', 'head')), parts along dimension 0, may hold values from -1 to 1023, as said below
- conv_weight: bfloat16 [27, 128, 128], replicated, may hold values from -0.15625 to 0.15625
- conv_bias: float32 [128], replicated, may hold values from -1.75 to 1.75
- cpe_weight: bfloat16 [128, 128], replicated, may hold values from -0.5 to 0.5
- cpe_bias: float32 [128], replicated, may hold values from -3 to 3
- norm_gain: float32 [3, 128], replicated, may hold values from 0.5 to 1.5
- norm_bias: float32 [3, 128], replicated, may hold values from -1.75 to 1.75
- qkv_weight: bfloat16 [128, 384], replicated
- qkv_bias: float32 [384], replicated, may hold values from -1.75 to 1.75
- proj_weight: bfloat16 [128, 128], replicated, may hold values from -0.5 to 0.5
- proj_bias: float32 [128], replicated, may hold values from -1.75 to 1.75
- fc1_weight: bfloat16 [128, 512], replicated, may hold values from -0.5 to 0.5
- fc1_bias: float32 [512], replicated, may hold values from -1.75 to 1.75
- fc2_weight: bfloat16 [512, 128], replicated, may hold values from -0.25 to 0.25
- fc2_bias: float32 [128], replicated, may hold values from -1.75 to 1.75
Outputs:
- block_out: bfloat16 [32768, 128], P(('groups', 'seg', 'head')), parts along dimension 0
The draws below stay inside these ranges and needn't reach their ends.
There are 2 independent parts, one for each index of `groups`. The reference program is written for one: setup_inputs(seed, part) draws one part's arguments, and reference() takes and returns one part's arrays. A program takes and returns all parts, laid end to end along the dimension named above; an argument that names none is the same for every part. Nothing has to cross between parts.
Inputs may be any that keep to these rules, and one draw needn't show every extreme that they name: `positions`: A permutation of the points. Points come in aligned runs of 16 consecutive z-order points that go to 16 consecutive places starting at a multiple of 16. The points of device d go only to the ranges of 1024 places of devices (d + s) mod 16 with s from -7 to 8, at most 128 places in the range of any one device, and every device sends exactly 128 to some device in every draw. `neighbors`: entry k = 13 of each row names the point itself. The coding of the other entries is that of the step neighbor_rows; every halo value names an entry t below the number of live entries of its list when that list's device exists. `send_rows`: row 4 * e + j lists distinct rows of device e that device e + b_j reads, b = (1, 2, -1, -2), followed by -1; each list holds 1 to 128 rows, and some list holds 128 in every draw.
All inputs are finite; a program needn't handle non-finite values.
Results may differ from the reference program's by a relative error of at most 0.007.
The reference program's roundings to bfloat16 on the way count: a program that leaves them out, or rounds other values in their place, can miss the bound.
Values may be sent and summed in bfloat16 or wider, within the bound.
A program may use at most 64 MiB of HBM per device.

```python
import jax
import jax.numpy as jnp
from jax import lax

C = 128
HEADS = 8
MLP_UNITS = 512
KERNEL = 27
PATCH = 1024
PEERS = 16
SEG_ROWS = 1024
HALO = 128
HEAD_DIM = 16
DEVS = 16
POINTS = 16384
UNIT = 16


def halo_lists(key):
    keys = jax.random.split(jax.random.fold_in(key, 21), 8)
    devices = POINTS // SEG_ROWS
    near_count = jax.random.randint(keys[0], (devices, 2), HALO // 2, HALO + 1)
    far_count = jax.random.randint(keys[1], (devices, 2), 1, HALO // 4 + 1)
    counts = jnp.stack([near_count[:, 0], far_count[:, 0], near_count[:, 1], far_count[:, 1]], axis=1)
    busiest = jax.random.randint(keys[2], (), 2, devices)
    list_index = jnp.arange(4)[None, :]
    forced = (jnp.arange(devices)[:, None] == busiest) & ((list_index == 0) | (list_index == 3))
    counts = jnp.where(forced, HALO, counts)
    quarter = SEG_ROWS // 4
    list_keys = jax.random.split(keys[3], devices * 4)
    picks = jax.vmap(lambda list_key: jax.random.permutation(list_key, quarter)[:HALO])(list_keys).reshape(devices, 4, HALO)
    picks = (picks - picks[:, :, :1]) % quarter
    from_end = jnp.array([1, 1, 0, 0], jnp.int32)[None, :, None] == 1
    chosen = jnp.where(from_end, SEG_ROWS - 1 - picks, picks)
    is_live = jnp.arange(HALO)[None, None, :] < counts[:, :, None]
    send = jnp.where(is_live, chosen, -1).reshape(devices * 4, HALO).astype(jnp.int32)
    row_ids = jnp.arange(SEG_ROWS)[None, :, None]
    device_ids = jnp.arange(devices)[:, None, None]
    grid_shape = (devices, SEG_ROWS, KERNEL)
    present = jax.random.randint(keys[4], grid_shape, 0, 8) < 5
    jitter = jax.random.randint(keys[5], grid_shape, -48, 49)
    local_ids = jnp.clip(row_ids + jitter, 0, SEG_ROWS - 1)
    coin = jax.random.randint(keys[6], grid_shape, 0, 8)
    edge_rows = SEG_ROWS // 8
    at_start = row_ids < edge_rows
    at_end = row_ids >= SEG_ROWS - edge_rows
    use_halo = (at_start | at_end) & (coin < 4)
    far_pick = coin == 0
    direction = jnp.where(at_start, jnp.where(far_pick, 1, 0), jnp.where(far_pick, 3, 2))
    offsets = jnp.array([1, 2, -1, -2], jnp.int32)
    source = jnp.clip(device_ids - offsets[direction], 0, devices - 1)
    available = counts[source, direction]
    slot_ids = jax.random.randint(keys[7], grid_shape, 0, HALO) % available
    halo_ids = SEG_ROWS + direction * HALO + slot_ids
    chosen_ids = jnp.where(use_halo, halo_ids, local_ids)
    centre = jnp.arange(KERNEL)[None, None, :] == KERNEL // 2
    neighbor_ids = jnp.where(centre, row_ids + 0 * chosen_ids, jnp.where(present, chosen_ids, -1))
    neighbor_ids = neighbor_ids.at[busiest - 2, SEG_ROWS - 1, 0].set(SEG_ROWS + 4 * HALO - 1)
    return (send, neighbor_ids.reshape(devices * SEG_ROWS, KERNEL).astype(jnp.int32))


def draw_send_rows(key, part):
    return halo_lists(key)[0]


def draw_neighbors(key, part):
    return halo_lists(key)[1]


def draw_positions(key, part):
    key = jax.random.fold_in(key, 7)
    key_swing, key_peer, key_source, key_dest = jax.random.split(key, 4)
    devices = POINTS // SEG_ROWS
    unit_count = SEG_ROWS // UNIT
    swing = jax.random.randint(key_swing, (PEERS // 2,), -4, 5)
    swing = swing.at[0].set(4)
    multiplicity = jnp.concatenate([4 + swing, 4 - swing])
    peer_shift = jax.random.permutation(key_peer, PEERS) - 7
    label_ends = jnp.cumsum(multiplicity)
    unit_ids = jnp.arange(unit_count)
    labels = jnp.sum((unit_ids[:, None] >= label_ends[None, :]).astype(jnp.int32), axis=1)
    source_order = jax.vmap(lambda order_key: jax.random.permutation(order_key, unit_count))(jax.random.split(key_source, devices))
    dest_order = jax.vmap(lambda order_key: jax.random.permutation(order_key, unit_count))(jax.random.split(key_dest, devices))
    device_ids = jnp.arange(devices)[:, None]
    dest_dev = (device_ids + peer_shift[labels[source_order]]) % devices
    slot_ids = dest_order[dest_dev, source_order]
    places = (dest_dev * SEG_ROWS + slot_ids * UNIT)[:, :, None] + jnp.arange(UNIT)[None, None, :]
    return places.reshape(-1).astype(jnp.int32)


def draw_qkv_weight(key, part):
    key = jax.random.fold_in(key, 5)
    base = jnp.clip(jax.random.normal(key, (C, 3 * C), jnp.float32), -4.5, 4.5) * C ** (-0.5)
    return base.astype(jnp.bfloat16)


def steps_of(rng, shape, pieces, low, top_value):
    gain = 1.0
    for dim, blocks in pieces:
        heights = jax.random.uniform(jax.random.fold_in(jax.random.fold_in(rng, 6), dim), (blocks,), jnp.float32, low / len(pieces), top_value / len(pieces))
        gain = gain * jnp.repeat(jnp.exp(heights), shape[dim] // blocks).reshape((-1,) + (1,) * (len(shape) - 1 - dim))
    return gain


def normal_values(own_key, shape, deviation, limit, cuts=(), kind=jnp.bfloat16):
    values = deviation * jax.random.normal(own_key, shape, jnp.float32)
    if cuts:
        values = values * steps_of(own_key, shape, cuts, -0.22, 0.18)
    return jnp.clip(values, -limit, limit).astype(kind)


def setup_inputs(seed: int = 0, part: int = 0) -> dict:
    splits = jax.random.split(jax.random.key(seed), 19)
    part_keys = jax.random.split(jax.random.fold_in(splits[18], part), 19)
    features = normal_values(part_keys[0], (POINTS, C), 1.0, 6.0, ((0, 16),))
    positions = draw_positions(jax.random.fold_in(jax.random.fold_in(splits[18], part), 71), part)
    neighbors = draw_neighbors(jax.random.fold_in(jax.random.fold_in(splits[18], part), 71), part)
    send_rows = draw_send_rows(jax.random.fold_in(jax.random.fold_in(splits[18], part), 71), part)
    conv_weight = normal_values(splits[4], (KERNEL, C, C), (KERNEL * C // 2) ** -0.5, 0.15625)
    conv_bias = normal_values(splits[5], (C,), 0.3, 1.75, (), jnp.float32)
    cpe_weight = normal_values(splits[6], (C, C), C ** -0.5, 0.5)
    cpe_bias = normal_values(splits[7], (C,), 0.5, 3.0, (), jnp.float32)
    norm_gain = jnp.clip(1.0 + 0.1 * jax.random.normal(splits[8], (3, C), jnp.float32), 0.5, 1.5)
    norm_bias = normal_values(splits[9], (3, C), 0.3, 1.75, (), jnp.float32)
    qkv_weight = draw_qkv_weight(jax.random.fold_in(splits[18], 71), part)
    qkv_bias = normal_values(splits[11], (3 * C,), 0.3, 1.75, (), jnp.float32)
    proj_weight = normal_values(splits[12], (C, C), C ** -0.5, 0.5)
    proj_bias = normal_values(splits[13], (C,), 0.3, 1.75, (), jnp.float32)
    fc1_weight = normal_values(splits[14], (C, MLP_UNITS), C ** -0.5, 0.5)
    fc1_bias = normal_values(splits[15], (MLP_UNITS,), 0.3, 1.75, (), jnp.float32)
    fc2_weight = normal_values(splits[16], (MLP_UNITS, C), MLP_UNITS ** -0.5, 0.25)
    fc2_bias = normal_values(splits[17], (C,), 0.3, 1.75, (), jnp.float32)
    return dict(features=features, positions=positions, neighbors=neighbors, send_rows=send_rows, conv_weight=conv_weight, conv_bias=conv_bias, cpe_weight=cpe_weight, cpe_bias=cpe_bias, norm_gain=norm_gain, norm_bias=norm_bias, qkv_weight=qkv_weight, qkv_bias=qkv_bias, proj_weight=proj_weight, proj_bias=proj_bias, fc1_weight=fc1_weight, fc1_bias=fc1_bias, fc2_weight=fc2_weight, fc2_bias=fc2_bias)


norm_epsilon = 1e-05
halo_offsets = (1, 2, -1, -2)

def normalize(values, norm_scale, norm_shift):
    row_mean = lax.optimization_barrier(jnp.mean(values, axis=-1, keepdims=True))
    centred = values - row_mean
    spread = lax.optimization_barrier(jnp.mean(centred * centred, axis=-1, keepdims=True))
    return centred * lax.rsqrt(spread + norm_epsilon) * norm_scale + norm_shift

def global_neighbors(neighbors, send_rows):
    device_ids = jnp.arange(DEVS, dtype=jnp.int32)
    table_parts = [device_ids[:, None] * SEG_ROWS + jnp.arange(SEG_ROWS, dtype=jnp.int32)[None, :]]
    lists = send_rows.reshape(DEVS, 4, HALO)
    for direction, offset in enumerate(halo_offsets):
        source = device_ids - offset
        has_source = (source >= 0) & (source < DEVS)
        clipped = jnp.clip(source, 0, DEVS - 1)
        picked = lists[clipped, direction]
        is_live = has_source[:, None] & (picked >= 0)
        table_parts.append(jnp.where(is_live, clipped[:, None] * SEG_ROWS + picked, -1))
    row_table = jnp.concatenate(table_parts, axis=1)
    local_ids = neighbors.reshape(DEVS, SEG_ROWS * KERNEL)
    global_ids = jnp.take_along_axis(row_table, jnp.maximum(local_ids, 0), axis=1)
    global_ids = jnp.where(local_ids >= 0, global_ids, -1)
    global_ids = jnp.where(global_ids < 0, POINTS, global_ids)
    return global_ids.reshape(POINTS, KERNEL).astype(jnp.int32)

def attend(joined_qkv):
    queries = joined_qkv[:, :C].reshape(PATCH, HEADS, HEAD_DIM).astype(jnp.float32)
    keys_all = joined_qkv[:, C:2 * C].reshape(PATCH, HEADS, HEAD_DIM).astype(jnp.float32)
    values_all = joined_qkv[:, 2 * C:].reshape(PATCH, HEADS, HEAD_DIM).astype(jnp.float32)
    scores = jnp.einsum('qhd,khd->hqk', queries, keys_all) * HEAD_DIM ** (-0.5)
    row_max = lax.optimization_barrier(jnp.max(scores, axis=-1, keepdims=True))
    exp_scores = jnp.exp(scores - row_max)
    weights = (exp_scores / lax.optimization_barrier(jnp.sum(exp_scores, axis=-1, keepdims=True))).astype(jnp.bfloat16)
    attended = jnp.einsum('hqk,khd->qhd', weights.astype(jnp.float32), values_all)
    return attended.reshape(PATCH, C).astype(jnp.bfloat16)

def reference(features, positions, neighbors, send_rows, conv_weight, conv_bias, cpe_weight, cpe_bias, norm_gain, norm_bias, qkv_weight, qkv_bias, proj_weight, proj_bias, fc1_weight, fc1_bias, fc2_weight, fc2_bias):
    global_ids = global_neighbors(neighbors, send_rows)
    padded = jnp.concatenate([features, jnp.zeros((1, C), features.dtype)], axis=0)
    flat_weight = conv_weight.reshape(KERNEL * C, C)
    block_rows = min(POINTS, 4096)

    def conv_block(block_ids):
        gathered = padded[block_ids].reshape(block_ids.shape[0], KERNEL * C)
        conv_part = jnp.dot(gathered, flat_weight, preferred_element_type=jnp.float32) + conv_bias
        return jnp.dot(conv_part.astype(jnp.bfloat16), cpe_weight, preferred_element_type=jnp.float32) + cpe_bias
    encoded = lax.map(conv_block, global_ids.reshape(POINTS // block_rows, block_rows, KERNEL)).reshape(POINTS, C)
    lifted = (features.astype(jnp.float32) + normalize(encoded, norm_gain[0], norm_bias[0])).astype(jnp.bfloat16)
    arranged = jnp.zeros((POINTS, C), jnp.bfloat16).at[positions].set(lifted)

    def patch_block(patch_rows):
        normed = normalize(patch_rows.astype(jnp.float32), norm_gain[1], norm_bias[1]).astype(jnp.bfloat16)
        joined_qkv = (jnp.dot(normed, qkv_weight, preferred_element_type=jnp.float32) + qkv_bias).astype(jnp.bfloat16)
        attended = attend(joined_qkv)
        residual_mid = patch_rows.astype(jnp.float32) + jnp.dot(attended, proj_weight, preferred_element_type=jnp.float32) + proj_bias
        normed_mid = normalize(residual_mid, norm_gain[2], norm_bias[2]).astype(jnp.bfloat16)
        hidden = jax.nn.gelu(jnp.dot(normed_mid, fc1_weight, preferred_element_type=jnp.float32) + fc1_bias, approximate=False).astype(jnp.bfloat16)
        return (residual_mid + jnp.dot(hidden, fc2_weight, preferred_element_type=jnp.float32) + fc2_bias).astype(jnp.bfloat16)
    block_out = lax.map(patch_block, arranged.reshape(POINTS // PATCH, PATCH, C))
    return block_out.reshape(POINTS, C)
```

```python
import functools
import math

import jax
import jax.numpy as jnp
from jax import lax
from jax.experimental import pallas as pl
from jax.experimental.pallas import tpu as pltpu
from jax.sharding import PartitionSpec as P

HEADS = 8
PEERS = 16
BACK = 7
UNITS_PER_PEER = 8
UNIT = 16

norm_epsilon = 1e-05
halo_offsets = (1, 2, -1, -2)
MESH = pl.DeviceIdType.MESH
VM = pl.BlockSpec(memory_space=pltpu.VMEM)
SM = pl.BlockSpec(memory_space=pltpu.SMEM)
f32 = jnp.float32
bf16 = jnp.bfloat16


def normalize(values, norm_scale, norm_shift):
    row_mean = jnp.mean(values, axis=-1, keepdims=True)
    centred = values - row_mean
    spread = jnp.mean(centred * centred, axis=-1, keepdims=True)
    return centred * lax.rsqrt(spread + norm_epsilon) * norm_scale + norm_shift


def dot(a, b):
    return jnp.dot(a, b, preferred_element_type=f32)


def place_of(cores):
    return lax.axis_index("seg") * cores + lax.axis_index("head")


def target(index, cores):
    return {"seg": index // cores, "head": lax.rem(index, cores)}


def greet(me, devs, cores):
    barrier = pltpu.get_barrier_semaphore()
    for label in range(PEERS):
        if label != BACK:
            sender = lax.rem(me - (label - BACK) + devs, devs)
            pl.semaphore_signal(
                barrier, inc=1, device_id=target(sender, cores), device_id_type=MESH
            )
    pl.semaphore_wait(barrier, PEERS - 1)


def halo_kernel(
    devs, cores, feat, picks, ucol, urow, halo, places, slots, outgoing, mine,
    landed, hs, hr, ps, pr,
):
    rows, channels = feat.shape
    width = picks.shape[0]
    me = place_of(cores)
    shift = int(math.log2(rows))
    units = ucol.shape[0]

    def labels(unit_places):
        lab = lax.shift_right_logical(unit_places, jnp.full_like(unit_places, shift)) - me + BACK
        lab = jnp.where(lab < 0, lab + devs, lab)
        return jnp.where(lab >= devs, lab - devs, lab)

    lab_col = labels(ucol[...])
    lab_row = labels(urow[...])
    first = lax.broadcasted_iota(jnp.int32, (units, units), 0)
    second = lax.broadcasted_iota(jnp.int32, (units, units), 1)
    rank = jnp.sum(jnp.where((lab_col == lab_row) & (first < second), 1, 0), axis=0, keepdims=True)
    slot = lab_row * UNITS_PER_PEER + rank
    slots[...] = slot
    slot_ids = lax.broadcasted_iota(jnp.int32, (PEERS * UNITS_PER_PEER, units), 0)
    own = jnp.sum(jnp.where(slot_ids == slot, urow[...] + 1, 0), axis=1, keepdims=True) - 1
    mine[...] = jnp.broadcast_to(own, mine.shape)

    row_ids = lax.broadcasted_iota(jnp.int32, (width, rows), 1)
    for j in range(4):
        table = (picks[:, j : j + 1] == row_ids).astype(f32).astype(bf16)
        outgoing[pl.ds(j * width, width), :] = dot(table, feat[...]).astype(bf16)

    greet(me, devs, cores)

    def halo_copy(j):
        part = pl.ds(j * width, width)
        there = jnp.clip(me + halo_offsets[j], 0, devs - 1)
        return pltpu.make_async_remote_copy(
            src_ref=outgoing.at[part], dst_ref=halo.at[part],
            send_sem=hs.at[j], recv_sem=hr.at[j],
            device_id=target(there, cores), device_id_type=MESH,
        )

    def place_copy(label):
        part = pl.ds(label * UNITS_PER_PEER, UNITS_PER_PEER)
        there = lax.rem(me + (label - BACK) + devs, devs)
        return pltpu.make_async_remote_copy(
            src_ref=mine.at[part], dst_ref=landed.at[part],
            send_sem=ps.at[label], recv_sem=pr.at[label],
            device_id=target(there, cores), device_id_type=MESH,
        )

    def sends(j):
        there = me + halo_offsets[j]
        return (there >= 0) & (there < devs)

    def receives(j):
        source = me - halo_offsets[j]
        return (source >= 0) & (source < devs)

    for j in range(4):
        pl.when(sends(j))(lambda j=j: halo_copy(j).start())
    for label in range(PEERS):
        if label != BACK:
            place_copy(label).start()
    home = pl.ds(BACK * UNITS_PER_PEER, UNITS_PER_PEER)
    landed[home, :] = mine[home, :]
    for j in range(4):
        part = pl.ds(j * width, width)

        @pl.when(jnp.logical_not(receives(j)))
        def _():
            halo[part, :] = jnp.zeros((width, channels), bf16)

    for j in range(4):
        pl.when(sends(j))(lambda j=j: halo_copy(j).wait_send())
        pl.when(receives(j))(lambda j=j: halo_copy(j).wait_recv())
    for label in range(PEERS):
        if label != BACK:
            place_copy(label).wait()
    arrived = landed[...]
    places[...] = jnp.where(arrived >= 0, arrived - me * rows, rows)


def swap_kernel(devs, cores, bucket, arrived, ss, rs, ls):
    me = place_of(cores)
    span = bucket.shape[0] // PEERS

    def copy(label):
        part = pl.ds(label * span, span)
        there = lax.rem(me + (label - BACK) + devs, devs)
        return pltpu.make_async_remote_copy(
            src_ref=bucket.at[part], dst_ref=arrived.at[part],
            send_sem=ss.at[label], recv_sem=rs.at[label],
            device_id=target(there, cores), device_id_type=MESH,
        )

    greet(me, devs, cores)
    others = [label for label in range(PEERS) if label != BACK]
    for label in others:
        copy(label).start()
    part = pl.ds(BACK * span, span)
    local = pltpu.make_async_copy(bucket.at[part], arrived.at[part], ls)
    local.start()
    local.wait()
    for label in others:
        copy(label).wait()


def conv_kernel(
    feat, halo, nbr, slots, conv_w, conv_b, cpe_w, cpe_b, gain, shift, bucket,
    table, acc, lifted,
):
    rows, channels = feat.shape
    taps = nbr.shape[1]
    total = rows + halo.shape[0]
    half = total // 2
    table[:, :channels] = feat[pl.ds(0, half), :]
    table[pl.ds(0, rows - half), channels:] = feat[pl.ds(half, rows - half), :]
    table[pl.ds(rows - half, total - rows), channels:] = halo[...]
    centre = taps // 2
    others = [k for k in range(taps) if k != centre]
    block = 512

    def row_block(b, carry):
        part = pl.ds(pl.multiple_of(b * block, block), block)
        lanes = lax.broadcasted_iota(jnp.int32, (block, half), 1)
        total_sum = dot(feat[part, :], conv_w[centre]) + conv_b[...]
        for n in range(0, len(others), 2):
            pair = []
            for k in others[n : n + 2]:
                ids = nbr[part, k : k + 1]
                upper = ids >= half
                local = jnp.where(upper, ids - half, ids)
                hot = (local == lanes).astype(f32).astype(bf16)
                both = dot(hot, table[...])
                pair.append(jnp.where(upper, both[:, channels:], both[:, :channels]).astype(bf16))
            weight = jnp.concatenate([conv_w[k] for k in others[n : n + 2]], axis=0)
            total_sum = total_sum + dot(jnp.concatenate(pair, axis=1), weight)
        encoded = dot(total_sum.astype(bf16), cpe_w[...]) + cpe_b[...]
        own = feat[part, :].astype(f32)
        lifted[part, :] = (own + normalize(encoded, gain[0:1, :], shift[0:1, :])).astype(bf16)
        return carry

    lax.fori_loop(0, rows // block, row_block, 0)
    bucket[...] = jnp.zeros_like(bucket)
    for u in range(rows // UNIT):
        slot = slots[0, u]
        bucket[pl.ds(pl.multiple_of(slot * UNIT, UNIT), UNIT), :] = lifted[pl.ds(u * UNIT, UNIT), :]


def patch_kernel(
    places, arrived, gain, shift, qkv_w, qkv_b, proj_w, proj_b, fc1_w, fc1_b,
    fc2_w, fc2_b, out, arranged, queries, keys, values,
):
    rows, channels = out.shape
    depth = channels // HEADS

    def put(s, carry):
        row = pl.multiple_of(places[s, 0], UNIT)
        arranged[pl.ds(row, UNIT), :] = arrived[pl.ds(pl.multiple_of(s * UNIT, UNIT), UNIT), :]
        return carry

    lax.fori_loop(0, PEERS * UNITS_PER_PEER, put, 0, unroll=8)
    source = arranged[pl.ds(0, rows), :].astype(f32)
    normed = normalize(source, gain[1:2, :], shift[1:2, :]).astype(bf16)
    joined = (dot(normed, qkv_w[...]) + qkv_b[...]).astype(bf16)
    queries[...] = (joined[:, :channels].astype(f32) * depth ** (-0.5)).astype(bf16)
    turned = jnp.transpose(joined[:, channels : 2 * channels].astype(f32))
    rows_of = lax.broadcasted_iota(jnp.int32, (channels, rows), 0) // depth
    vals = joined[:, 2 * channels :].astype(f32)
    lanes_of = lax.broadcasted_iota(jnp.int32, (rows, channels), 1) // depth
    for h in range(HEADS):
        keys[h] = jnp.where(rows_of == h, turned, 0.0).astype(bf16)
        values[h, :, :channels] = jnp.where(lanes_of == h, vals, 0.0).astype(bf16)
        values[h, :, channels:] = jnp.where(lanes_of == h, 1.0, 0.0).astype(bf16)
    block = 256

    def row_block(b, carry):
        part = pl.ds(pl.multiple_of(b * block, block), block)
        query = queries[part, :]
        sums = jnp.zeros((block, 2 * channels), f32)
        for h in range(HEADS):
            scores = dot(query, keys[h])
            row_max = jnp.max(scores, axis=-1, keepdims=True)
            weights = jnp.exp(scores - row_max).astype(bf16)
            sums = sums + dot(weights, values[h])
        attended = (sums[:, :channels] / sums[:, channels:]).astype(bf16)
        middle = arranged[part, :].astype(f32) + dot(attended, proj_w[...]) + proj_b[...]
        normed_mid = normalize(middle, gain[2:3, :], shift[2:3, :]).astype(bf16)
        raw = dot(normed_mid, fc1_w[...]) + fc1_b[...]
        hidden = (0.5 * raw * (1.0 + lax.erf(raw * (0.5 ** 0.5)))).astype(bf16)
        out[part, :] = (middle + dot(hidden, fc2_w[...]) + fc2_b[...]).astype(bf16)
        return carry

    lax.fori_loop(0, rows // block, row_block, 0)


def per_device(
    features, positions, neighbors, send_rows, conv_weight, conv_bias, cpe_weight,
    cpe_bias, norm_gain, norm_bias, qkv_weight, qkv_bias, proj_weight, proj_bias,
    fc1_weight, fc1_bias, fc2_weight, fc2_bias,
):
    rows, channels = features.shape
    cores = lax.axis_size("head")
    devs = lax.axis_size("seg") * cores
    width = send_rows.shape[1]
    units = rows // UNIT
    slot_count = PEERS * UNITS_PER_PEER
    dma = pltpu.SemaphoreType.DMA
    unit_places = positions.reshape(units, UNIT)[:, 0]
    limit = 48 * 1024 * 1024

    halo, places, slots = pl.pallas_call(
        functools.partial(halo_kernel, devs, cores),
        out_shape=(
            jax.ShapeDtypeStruct((4 * width, channels), bf16),
            jax.ShapeDtypeStruct((slot_count, 128), jnp.int32),
            jax.ShapeDtypeStruct((1, units), jnp.int32),
        ),
        in_specs=[VM] * 4,
        out_specs=(VM, VM, VM),
        scratch_shapes=[
            pltpu.VMEM((4 * width, channels), bf16),
            pltpu.VMEM((slot_count, 128), jnp.int32),
            pltpu.VMEM((slot_count, 128), jnp.int32),
            dma((4,)), dma((4,)), dma((PEERS,)), dma((PEERS,)),
        ],
        compiler_params=pltpu.CompilerParams(
            collective_id=0, has_side_effects=True, vmem_limit_bytes=limit
        ),
        name="halo",
    )(features, send_rows.T, unit_places[:, None], unit_places[None, :])

    bucket = pl.pallas_call(
        conv_kernel,
        out_shape=jax.ShapeDtypeStruct((slot_count * UNIT, channels), bf16),
        in_specs=[VM, VM, VM, SM] + [VM] * 6,
        out_specs=VM,
        scratch_shapes=[
            pltpu.VMEM(((rows + 4 * width) // 2, 2 * channels), bf16),
            pltpu.VMEM((rows, channels), f32),
            pltpu.VMEM((rows, channels), bf16),
        ],
        compiler_params=pltpu.CompilerParams(vmem_limit_bytes=limit),
        name="conv",
    )(
        features, halo, neighbors, slots, conv_weight, conv_bias[None], cpe_weight,
        cpe_bias[None], norm_gain, norm_bias,
    )

    arrived = pl.pallas_call(
        functools.partial(swap_kernel, devs, cores),
        out_shape=jax.ShapeDtypeStruct(bucket.shape, bf16),
        in_specs=[VM],
        out_specs=VM,
        scratch_shapes=[dma((PEERS,)), dma((PEERS,)), dma],
        compiler_params=pltpu.CompilerParams(
            collective_id=1, has_side_effects=True, vmem_limit_bytes=limit
        ),
        name="swap",
    )(bucket)

    return pl.pallas_call(
        patch_kernel,
        out_shape=jax.ShapeDtypeStruct((rows, channels), bf16),
        in_specs=[SM] + [VM] * 11,
        out_specs=VM,
        scratch_shapes=[
            pltpu.VMEM((rows + UNIT, channels), bf16),
            pltpu.VMEM((rows, channels), bf16),
            pltpu.VMEM((HEADS, channels, rows), bf16),
            pltpu.VMEM((HEADS, rows, 2 * channels), bf16),
        ],
        compiler_params=pltpu.CompilerParams(vmem_limit_bytes=limit),
        name="patch",
    )(
        places, arrived, norm_gain, norm_bias, qkv_weight, qkv_bias[None], proj_weight,
        proj_bias[None], fc1_weight, fc1_bias[None], fc2_weight, fc2_bias[None],
    )


def solution(mesh):
    split = P(("groups", "seg", "head"), None)
    placed = (split, P(("groups", "seg", "head")), split, split) + (P(),) * 14
    return jax.shard_map(
        per_device, mesh=mesh, in_specs=placed, out_specs=split, check_vma=False
    )
```

```python
import functools
import math

import jax
import jax.numpy as jnp
from jax import lax
from jax.experimental import pallas as pl
from jax.experimental.pallas import tpu as pltpu
from jax.sharding import PartitionSpec as P

HEADS = 8
PEERS = 16
BACK = 7
UNITS_PER_PEER = 8
UNIT = 16

norm_epsilon = 1e-05
halo_offsets = (1, 2, -1, -2)
MESH = pl.DeviceIdType.MESH
VM = pl.BlockSpec(memory_space=pltpu.VMEM)
SM = pl.BlockSpec(memory_space=pltpu.SMEM)
f32 = jnp.float32
bf16 = jnp.bfloat16


def normalize(values, norm_scale, norm_shift):
    row_mean = jnp.mean(values, axis=-1, keepdims=True)
    centred = values - row_mean
    spread = jnp.mean(centred * centred, axis=-1, keepdims=True)
    return centred * lax.rsqrt(spread + norm_epsilon) * norm_scale + norm_shift


def dot(a, b):
    return jnp.dot(a, b, preferred_element_type=f32)


def place_of(cores):
    return lax.axis_index("seg") * cores + lax.axis_index("head")


def target(index, cores):
    return {"seg": index // cores, "head": lax.rem(index, cores)}


def ahead(me, step, devs):
    if devs == PEERS:
        half = devs // 2
        mine = me // half
        across = (1 - mine) * half + lax.rem(me + step, half)
        beside = mine * half + lax.rem(me + step + 1, half)
        return jnp.where(step < half, across, beside)
    return lax.rem(me + jnp.where(step < PEERS // 2, PEERS // 2 - step, PEERS // 2 - 1 - step + devs)
                   + jnp.where(step == PEERS - 1, PEERS // 2 , 0), devs)


def step_of(dest, me, devs):
    if devs == PEERS:
        half = devs // 2
        far = (dest >= half) != (me >= half)
        gap = dest - me
        return jnp.where(far, (gap + devs) & (half - 1), half + ((gap - 1 + devs) & (half - 1)))
    gap = dest - me
    gap = jnp.where(gap < -BACK, gap + devs, gap)
    gap = jnp.where(gap > PEERS // 2, gap - devs, gap)
    return jnp.where(gap > 0, PEERS // 2 - gap, jnp.where(gap == 0, PEERS - 1, PEERS // 2 - 1 - gap))


def label_of(dest, me, devs):
    return lax.rem(dest - me + BACK + devs, devs)


def conv_kernel(
    devs, cores, feat, picks, ucol, urow, prow, nbr, conv_w, conv_b, cpe_w, cpe_b, gain, shift,
    arrived, places, halo, outgoing, mine, landed, bucket, table, wide, cols, uppers, own,
    acc, lifted, hs, hr, ps, pr, ss, rs,
):
    rows, channels = feat.shape
    width = picks.shape[0]
    units = ucol.shape[0]
    taps = nbr.shape[1]
    me = place_of(cores)
    log_rows = int(math.log2(rows))
    log_unit = int(math.log2(UNIT))
    span = UNITS_PER_PEER * UNIT
    half = rows // 2

    barrier = pltpu.get_barrier_semaphore()
    for label in range(PEERS):
        if label != BACK:
            sender = lax.rem(me - (label - BACK) + devs, devs)
            pl.semaphore_signal(
                barrier, inc=1, device_id=target(sender, cores), device_id_type=MESH
            )

    def steps(unit_places):
        return step_of(lax.shift_right_logical(unit_places, jnp.full_like(unit_places, log_rows)), me, devs)

    step_col = steps(ucol[...])
    step_row = steps(urow[...])
    first = lax.broadcasted_iota(jnp.int32, (units, units), 0)
    second = lax.broadcasted_iota(jnp.int32, (units, units), 1)
    rank = jnp.sum(jnp.where((step_col == step_row) & (first < second), 1, 0), axis=0, keepdims=True)
    slot = step_row * UNITS_PER_PEER + rank
    slot_ids = lax.broadcasted_iota(jnp.int32, (PEERS * UNITS_PER_PEER, units), 0)
    sent = jnp.sum(jnp.where(slot_ids == slot, urow[...] + 1, 0), axis=1, keepdims=True) - 1
    mine[...] = jnp.broadcast_to(sent, mine.shape)

    row_ids = lax.broadcasted_iota(jnp.int32, (width, rows), 1)
    for j in range(4):
        hot = (picks[:, j : j + 1] == row_ids).astype(f32).astype(bf16)
        outgoing[pl.ds(j * width, width), :] = dot(hot, feat[...]).astype(bf16)

    def halo_copy(j):
        part = pl.ds(j * width, width)
        there = jnp.clip(me + halo_offsets[j], 0, devs - 1)
        return pltpu.make_async_remote_copy(
            src_ref=outgoing.at[part], dst_ref=halo.at[part],
            send_sem=hs.at[j], recv_sem=hr.at[j],
            device_id=target(there, cores), device_id_type=MESH,
        )

    def sends(j):
        there = me + halo_offsets[j]
        return (there >= 0) & (there < devs)

    def receives(j):
        source = me - halo_offsets[j]
        return (source >= 0) & (source < devs)

    def place_copy(step, label=None):
        there = ahead(me, step, devs)
        label = label_of(there, me, devs) if label is None else label
        return pltpu.make_async_remote_copy(
            src_ref=mine.at[pl.ds(pl.multiple_of(step * UNITS_PER_PEER, UNITS_PER_PEER), UNITS_PER_PEER)],
            dst_ref=landed.at[pl.ds(pl.multiple_of(label * UNITS_PER_PEER, UNITS_PER_PEER), UNITS_PER_PEER)],
            send_sem=ps.at[step], recv_sem=pr.at[label],
            device_id=target(there, cores), device_id_type=MESH,
        )

    def row_copy(step, label=None):
        there = ahead(me, step, devs)
        label = label_of(there, me, devs) if label is None else label
        return pltpu.make_async_remote_copy(
            src_ref=bucket.at[pl.ds(pl.multiple_of(step * span, span), span)],
            dst_ref=arrived.at[pl.ds(pl.multiple_of(label * span, span), span)],
            send_sem=ss.at[step], recv_sem=rs.at[label],
            device_id=target(there, cores), device_id_type=MESH,
        )

    pl.semaphore_wait(barrier, PEERS - 1)
    for j in range(4):
        pl.when(sends(j))(lambda j=j: halo_copy(j).start())
    for step in range(PEERS - 1):
        place_copy(jnp.int32(step)).start()

    table[pl.ds(0, half), :channels] = feat[pl.ds(0, half), :]
    table[pl.ds(0, half), channels:] = feat[pl.ds(half, half), :]
    lifted[...] = jnp.zeros_like(lifted)

    row_steps = steps(prow[...])
    unit_of = lax.shift_right_logical(
        lax.broadcasted_iota(jnp.int32, (1, rows), 1), jnp.full((1, rows), log_unit, jnp.int32)
    )
    unit_col = lax.broadcasted_iota(jnp.int32, (units, 1), 0)
    before = (step_col < row_steps) | ((step_col == row_steps) & (unit_col < unit_of))
    rank_row = jnp.sum(jnp.where(before, 1, 0), axis=0, keepdims=True)
    dest_row = rank_row * UNIT + (lax.broadcasted_iota(jnp.int32, (1, rows), 1) & (UNIT - 1))
    codes = nbr[...] + 1
    high = lax.shift_right_logical(codes, jnp.full_like(codes, 5))
    wide[:, :channels] = feat[...]
    wide[:, channels:] = jnp.zeros((rows, channels), bf16)
    wide[:, channels : channels + taps] = high.astype(f32).astype(bf16)
    wide[:, channels + 32 : channels + 32 + taps] = (codes & 31).astype(f32).astype(bf16)
    sort = (lax.broadcasted_iota(jnp.int32, (rows, rows), 0) == dest_row).astype(f32).astype(bf16)
    ordered = dot(sort, wide[...])
    own[...] = ordered[:, :channels].astype(bf16)
    ids = (
        ordered[:, channels : channels + 32] * 32.0 + ordered[:, channels + 32 : channels + 64] - 1.0
    ).astype(jnp.int32)
    away = ids >= rows
    upper = (ids >= rows + 2 * width) | ((ids >= half) & (ids < rows))
    cols[...] = jnp.where(
        away,
        half + ids - rows - jnp.where(upper, 2 * width, 0),
        ids - jnp.where(upper, half, 0),
    )
    uppers[...] = jnp.where(upper, 1, 0)

    centre = taps // 2
    others = [k for k in range(taps) if k != centre]
    block = 256
    group = 2

    def conv_pass(b, base, depth, start):
        part = pl.ds(pl.multiple_of(b * block, block), block)
        lanes = lax.broadcasted_iota(jnp.int32, (block, depth), 1) + base
        total = start
        for n in range(0, len(others), group):
            ks = others[n : n + group]
            hot = jnp.concatenate(
                [(cols[part, k : k + 1] == lanes).astype(f32).astype(bf16) for k in ks], axis=0
            )
            both = dot(hot, table[pl.ds(base, depth), :])
            chosen = []
            for i, k in enumerate(ks):
                piece = both[i * block : (i + 1) * block]
                chosen.append(
                    jnp.where(uppers[part, k : k + 1] > 0, piece[:, channels:], piece[:, :channels]).astype(bf16)
                )
            weight = jnp.concatenate([conv_w[k] for k in ks], axis=0)
            total = total + dot(jnp.concatenate(chosen, axis=1), weight)
        return total

    def begun(b):
        part = pl.ds(pl.multiple_of(b * block, block), block)
        return dot(own[part, :], conv_w[centre]) + conv_b[...]

    def local_block(b, carry):
        acc[pl.ds(pl.multiple_of(b * block, block), block), :] = conv_pass(b, 0, half, begun(b))
        return carry

    def pack(start, count):
        slot_rows = count * span
        q = lax.broadcasted_iota(jnp.int32, (slot_rows, 1), 0) + start * span
        step = lax.shift_right_logical(q, jnp.full_like(q, int(math.log2(span))))
        smaller = jnp.sum(jnp.where(step_row < step, 1, 0), axis=1, keepdims=True)
        source = smaller * UNIT + (q & (span - 1))
        hot = (source == lax.broadcasted_iota(jnp.int32, (slot_rows, rows), 1)).astype(f32).astype(bf16)
        return dot(hot, lifted[...]).astype(bf16)

    def finish(b, total):
        part = pl.ds(pl.multiple_of(b * block, block), block)
        encoded = dot(total.astype(bf16), cpe_w[...]) + cpe_b[...]
        lifted[part, :] = (
            own[part, :].astype(f32) + normalize(encoded, gain[0:1, :], shift[0:1, :])
        ).astype(bf16)
        per = block // span
        bucket[pl.ds(pl.multiple_of(b * block, block), block), :] = pack(b * per, per)
        for i in range(per):
            row_copy(b * per + i).start()

    def halo_block(b, carry):
        part = pl.ds(pl.multiple_of(b * block, block), block)
        finish(b, conv_pass(b, half, 2 * width, acc[part, :]))
        return carry

    def full_block(b, carry):
        finish(b, conv_pass(b, 0, half + 2 * width, begun(b)))
        return carry

    lax.fori_loop(0, 2, local_block, 0)
    for j in range(4):
        pl.when(sends(j))(lambda j=j: halo_copy(j).wait_send())
        pl.when(receives(j))(lambda j=j: halo_copy(j).wait_recv())
        landing = pl.ds(half + (j % 2) * width, width)
        lane_part = pl.ds((j // 2) * channels, channels)

        @pl.when(receives(j))
        def _():
            table[landing, lane_part] = halo[pl.ds(j * width, width), :]

        @pl.when(jnp.logical_not(receives(j)))
        def _():
            table[landing, lane_part] = jnp.zeros((width, channels), bf16)

    lax.fori_loop(0, 2, halo_block, 0)
    lax.fori_loop(2, rows // block, full_block, 0)
    done = rows // span
    rest = pack(done, PEERS - done)
    bucket[pl.ds(rows, (PEERS - done) * span), :] = rest
    for step in range(done, PEERS - 1):
        row_copy(jnp.int32(step)).start()
    arrived[pl.ds(BACK * span, span), :] = bucket[pl.ds((PEERS - 1) * span, span), :]
    home = pl.ds(BACK * UNITS_PER_PEER, UNITS_PER_PEER)
    landed[home, :] = mine[pl.ds((PEERS - 1) * UNITS_PER_PEER, UNITS_PER_PEER), :]
    for step in range(PEERS - 1):
        place_copy(jnp.int32(step)).wait_send()
        row_copy(jnp.int32(step)).wait_send()
    for label in range(PEERS):
        if label != BACK:
            place_copy(jnp.int32(0), label).wait_recv()
            row_copy(jnp.int32(0), label).wait_recv()
    seen = landed[...]
    places[...] = jnp.where(seen >= 0, seen - me * rows, rows)


def patch_kernel(
    places, arrived, gain, shift, qkv_w, qkv_b, proj_w, proj_b, fc1_w, fc1_b,
    fc2_w, fc2_b, out, arranged, queries, keys, values,
):
    rows, channels = out.shape
    depth = channels // HEADS

    def put(s, carry):
        row = pl.multiple_of(places[s, 0], UNIT)
        arranged[pl.ds(row, UNIT), :] = arrived[pl.ds(pl.multiple_of(s * UNIT, UNIT), UNIT), :]
        return carry

    lax.fori_loop(0, PEERS * UNITS_PER_PEER, put, 0, unroll=8)
    source = arranged[pl.ds(0, rows), :].astype(f32)
    normed = normalize(source, gain[1:2, :], shift[1:2, :]).astype(bf16)
    joined = (dot(normed, qkv_w[...]) + qkv_b[...]).astype(bf16)
    queries[...] = (joined[:, :channels].astype(f32) * depth ** (-0.5)).astype(bf16)
    turned = jnp.transpose(joined[:, channels : 2 * channels].astype(f32))
    rows_of = lax.broadcasted_iota(jnp.int32, (channels, rows), 0) // depth
    vals = joined[:, 2 * channels :].astype(f32)
    lanes_of = lax.broadcasted_iota(jnp.int32, (rows, channels), 1) // depth
    for h in range(HEADS):
        keys[h] = jnp.where(rows_of == h, turned, 0.0).astype(bf16)
        values[h, :, :channels] = jnp.where(lanes_of == h, vals, 0.0).astype(bf16)
        values[h, :, channels:] = jnp.where(lanes_of == h, 1.0, 0.0).astype(bf16)
    block = 1024

    def row_block(b, carry):
        part = pl.ds(pl.multiple_of(b * block, block), block)
        query = queries[part, :]
        sums = jnp.zeros((block, 2 * channels), f32)
        for h in range(HEADS):
            scores = dot(query, keys[h])
            row_max = jnp.max(scores, axis=-1, keepdims=True)
            weights = jnp.exp(scores - row_max).astype(bf16)
            sums = sums + dot(weights, values[h])
        attended = (sums[:, :channels] / sums[:, channels:]).astype(bf16)
        middle = arranged[part, :].astype(f32) + dot(attended, proj_w[...]) + proj_b[...]
        normed_mid = normalize(middle, gain[2:3, :], shift[2:3, :]).astype(bf16)
        raw = dot(normed_mid, fc1_w[...]) + fc1_b[...]
        hidden = (0.5 * raw * (1.0 + lax.erf(raw * (0.5 ** 0.5)))).astype(bf16)
        out[part, :] = (middle + dot(hidden, fc2_w[...]) + fc2_b[...]).astype(bf16)
        return carry

    lax.fori_loop(0, rows // block, row_block, 0)


def per_device(
    features, positions, neighbors, send_rows, conv_weight, conv_bias, cpe_weight,
    cpe_bias, norm_gain, norm_bias, qkv_weight, qkv_bias, proj_weight, proj_bias,
    fc1_weight, fc1_bias, fc2_weight, fc2_bias,
):
    rows, channels = features.shape
    cores = lax.axis_size("head")
    devs = lax.axis_size("seg") * cores
    width = send_rows.shape[1]
    units = rows // UNIT
    slot_count = PEERS * UNITS_PER_PEER
    dma = pltpu.SemaphoreType.DMA
    unit_places = positions.reshape(units, UNIT)[:, 0]
    limit = 48 * 1024 * 1024

    i32 = jnp.int32
    arrived, places = pl.pallas_call(
        functools.partial(conv_kernel, devs, cores),
        out_shape=(
            jax.ShapeDtypeStruct((slot_count * UNIT, channels), bf16),
            jax.ShapeDtypeStruct((slot_count, 128), i32),
        ),
        in_specs=[VM] * 12,
        out_specs=(VM, VM),
        scratch_shapes=[
            pltpu.VMEM((4 * width, channels), bf16),
            pltpu.VMEM((4 * width, channels), bf16),
            pltpu.VMEM((slot_count, 128), i32),
            pltpu.VMEM((slot_count, 128), i32),
            pltpu.VMEM((slot_count * UNIT, channels), bf16),
            pltpu.VMEM(((rows + 4 * width) // 2, 2 * channels), bf16),
            pltpu.VMEM((rows, 2 * channels), bf16),
            pltpu.VMEM((rows, 32), i32),
            pltpu.VMEM((rows, 32), i32),
            pltpu.VMEM((rows, channels), bf16),
            pltpu.VMEM((rows, channels), f32),
            pltpu.VMEM((rows, channels), bf16),
            dma((4,)), dma((4,)), dma((PEERS,)), dma((PEERS,)), dma((PEERS,)), dma((PEERS,)),
        ],
        compiler_params=pltpu.CompilerParams(
            collective_id=0, has_side_effects=True, vmem_limit_bytes=limit
        ),
        name="conv",
    )(
        features, send_rows.T, unit_places[:, None], unit_places[None, :], positions[None, :],
        neighbors, conv_weight, conv_bias[None], cpe_weight, cpe_bias[None], norm_gain, norm_bias,
    )

    return pl.pallas_call(
        patch_kernel,
        out_shape=jax.ShapeDtypeStruct((rows, channels), bf16),
        in_specs=[SM] + [VM] * 11,
        out_specs=VM,
        scratch_shapes=[
            pltpu.VMEM((rows + UNIT, channels), bf16),
            pltpu.VMEM((rows, channels), bf16),
            pltpu.VMEM((HEADS, channels, rows), bf16),
            pltpu.VMEM((HEADS, rows, 2 * channels), bf16),
        ],
        compiler_params=pltpu.CompilerParams(vmem_limit_bytes=limit),
        name="patch",
    )(
        places, arrived, norm_gain, norm_bias, qkv_weight, qkv_bias[None], proj_weight,
        proj_bias[None], fc1_weight, fc1_bias[None], fc2_weight, fc2_bias[None],
    )


def solution(mesh):
    split = P(("groups", "seg", "head"), None)
    placed = (split, P(("groups", "seg", "head")), split, split) + (P(),) * 14
    return jax.shard_map(
        per_device, mesh=mesh, in_specs=placed, out_specs=split, check_vma=False
    )
```

```python
import functools
import math

import jax
import jax.numpy as jnp
from jax import lax
from jax.experimental import pallas as pl
from jax.experimental.pallas import tpu as pltpu
from jax.sharding import PartitionSpec as P

HEADS = 8
PEERS = 16
BACK = 7
UNITS_PER_PEER = 8
UNIT = 16

norm_epsilon = 1e-05
halo_offsets = (1, 2, -1, -2)
MESH = pl.DeviceIdType.MESH
VM = pl.BlockSpec(memory_space=pltpu.VMEM)
SM = pl.BlockSpec(memory_space=pltpu.SMEM)
f32 = jnp.float32
bf16 = jnp.bfloat16


def normalize(values, norm_scale, norm_shift):
    row_mean = jnp.mean(values, axis=-1, keepdims=True)
    centred = values - row_mean
    spread = jnp.mean(centred * centred, axis=-1, keepdims=True)
    return centred * lax.rsqrt(spread + norm_epsilon) * norm_scale + norm_shift


def dot(a, b):
    return jnp.dot(a, b, preferred_element_type=f32)


def place_of(cores):
    return lax.axis_index("seg") * cores + lax.axis_index("head")


def target(index, cores):
    return {"seg": index // cores, "head": lax.rem(index, cores)}


def greet(me, devs, cores):
    barrier = pltpu.get_barrier_semaphore()
    for label in range(PEERS):
        if label != BACK:
            sender = lax.rem(me - (label - BACK) + devs, devs)
            pl.semaphore_signal(
                barrier, inc=1, device_id=target(sender, cores), device_id_type=MESH
            )
    pl.semaphore_wait(barrier, PEERS - 1)


def halo_kernel(
    devs, cores, feat, picks, ucol, urow, halo, places, slots, outgoing, mine,
    landed, hs, hr, ps, pr,
):
    rows, channels = feat.shape
    width = picks.shape[0]
    me = place_of(cores)
    shift = int(math.log2(rows))
    units = ucol.shape[0]

    def labels(unit_places):
        lab = lax.shift_right_logical(unit_places, jnp.full_like(unit_places, shift)) - me + BACK
        lab = jnp.where(lab < 0, lab + devs, lab)
        return jnp.where(lab >= devs, lab - devs, lab)

    lab_col = labels(ucol[...])
    lab_row = labels(urow[...])
    first = lax.broadcasted_iota(jnp.int32, (units, units), 0)
    second = lax.broadcasted_iota(jnp.int32, (units, units), 1)
    rank = jnp.sum(jnp.where((lab_col == lab_row) & (first < second), 1, 0), axis=0, keepdims=True)
    slot = lab_row * UNITS_PER_PEER + rank
    slots[...] = slot
    slot_ids = lax.broadcasted_iota(jnp.int32, (PEERS * UNITS_PER_PEER, units), 0)
    own = jnp.sum(jnp.where(slot_ids == slot, urow[...] + 1, 0), axis=1, keepdims=True) - 1
    mine[...] = jnp.broadcast_to(own, mine.shape)

    row_ids = lax.broadcasted_iota(jnp.int32, (width, rows), 1)
    for j in range(4):
        table = (picks[:, j : j + 1] == row_ids).astype(f32).astype(bf16)
        outgoing[pl.ds(j * width, width), :] = dot(table, feat[...]).astype(bf16)

    greet(me, devs, cores)

    def halo_copy(j):
        part = pl.ds(j * width, width)
        there = jnp.clip(me + halo_offsets[j], 0, devs - 1)
        return pltpu.make_async_remote_copy(
            src_ref=outgoing.at[part], dst_ref=halo.at[part],
            send_sem=hs.at[j], recv_sem=hr.at[j],
            device_id=target(there, cores), device_id_type=MESH,
        )

    def place_copy(label):
        part = pl.ds(label * UNITS_PER_PEER, UNITS_PER_PEER)
        there = lax.rem(me + (label - BACK) + devs, devs)
        return pltpu.make_async_remote_copy(
            src_ref=mine.at[part], dst_ref=landed.at[part],
            send_sem=ps.at[label], recv_sem=pr.at[label],
            device_id=target(there, cores), device_id_type=MESH,
        )

    def sends(j):
        there = me + halo_offsets[j]
        return (there >= 0) & (there < devs)

    def receives(j):
        source = me - halo_offsets[j]
        return (source >= 0) & (source < devs)

    for j in range(4):
        pl.when(sends(j))(lambda j=j: halo_copy(j).start())
    for label in range(PEERS):
        if label != BACK:
            place_copy(label).start()
    home = pl.ds(BACK * UNITS_PER_PEER, UNITS_PER_PEER)
    landed[home, :] = mine[home, :]
    for j in range(4):
        part = pl.ds(j * width, width)

        @pl.when(jnp.logical_not(receives(j)))
        def _():
            halo[part, :] = jnp.zeros((width, channels), bf16)

    for j in range(4):
        pl.when(sends(j))(lambda j=j: halo_copy(j).wait_send())
        pl.when(receives(j))(lambda j=j: halo_copy(j).wait_recv())
    for label in range(PEERS):
        if label != BACK:
            place_copy(label).wait()
    arrived = landed[...]
    places[...] = jnp.where(arrived >= 0, arrived - me * rows, rows)


def ahead(me, step, devs):
    if devs == PEERS:
        half = devs // 2
        mine = me // half
        across = (1 - mine) * half + lax.rem(me + step, half)
        beside = mine * half + lax.rem(me + step + 1, half)
        return jnp.where(step < half, across, beside)
    return lax.rem(me + jnp.where(step < PEERS // 2, PEERS // 2 - step, PEERS // 2 - 1 - step + devs)
                   + jnp.where(step == PEERS - 1, PEERS // 2 , 0), devs)


def label_of(dest, me, devs):
    return lax.rem(dest - me + BACK + devs, devs)


def swap_kernel(devs, cores, bucket, arrived, ss, rs, ls):
    me = place_of(cores)
    span = bucket.shape[0] // PEERS

    def copy(label):
        part = pl.ds(pl.multiple_of(label * span, span), span)
        there = lax.rem(me + (label - BACK) + devs, devs)
        return pltpu.make_async_remote_copy(
            src_ref=bucket.at[part], dst_ref=arrived.at[part],
            send_sem=ss.at[label], recv_sem=rs.at[label],
            device_id=target(there, cores), device_id_type=MESH,
        )

    greet(me, devs, cores)
    others = [label for label in range(PEERS) if label != BACK]
    for step in range(PEERS - 1):
        copy(label_of(ahead(me, jnp.int32(step), devs), me, devs)).start()
    part = pl.ds(BACK * span, span)
    local = pltpu.make_async_copy(bucket.at[part], arrived.at[part], ls)
    local.start()
    local.wait()
    for label in others:
        copy(label).wait()


def conv_kernel(
    feat, halo, nbr, slots, conv_w, conv_b, cpe_w, cpe_b, gain, shift, bucket,
    table, acc, lifted,
):
    rows, channels = feat.shape
    taps = nbr.shape[1]
    total = rows + halo.shape[0]
    half = total // 2
    table[:, :channels] = feat[pl.ds(0, half), :]
    table[pl.ds(0, rows - half), channels:] = feat[pl.ds(half, rows - half), :]
    table[pl.ds(rows - half, total - rows), channels:] = halo[...]
    centre = taps // 2
    others = [k for k in range(taps) if k != centre]
    block = 512

    def row_block(b, carry):
        part = pl.ds(pl.multiple_of(b * block, block), block)
        lanes = lax.broadcasted_iota(jnp.int32, (block, half), 1)
        total_sum = dot(feat[part, :], conv_w[centre]) + conv_b[...]
        for n in range(0, len(others), 2):
            pair = []
            for k in others[n : n + 2]:
                ids = nbr[part, k : k + 1]
                upper = ids >= half
                local = jnp.where(upper, ids - half, ids)
                hot = (local == lanes).astype(f32).astype(bf16)
                both = dot(hot, table[...])
                pair.append(jnp.where(upper, both[:, channels:], both[:, :channels]).astype(bf16))
            weight = jnp.concatenate([conv_w[k] for k in others[n : n + 2]], axis=0)
            total_sum = total_sum + dot(jnp.concatenate(pair, axis=1), weight)
        encoded = dot(total_sum.astype(bf16), cpe_w[...]) + cpe_b[...]
        own = feat[part, :].astype(f32)
        lifted[part, :] = (own + normalize(encoded, gain[0:1, :], shift[0:1, :])).astype(bf16)
        return carry

    lax.fori_loop(0, rows // block, row_block, 0)
    bucket[...] = jnp.zeros_like(bucket)
    for u in range(rows // UNIT):
        slot = slots[0, u]
        bucket[pl.ds(pl.multiple_of(slot * UNIT, UNIT), UNIT), :] = lifted[pl.ds(u * UNIT, UNIT), :]


def patch_kernel(
    places, arrived, gain, shift, qkv_w, qkv_b, proj_w, proj_b, fc1_w, fc1_b,
    fc2_w, fc2_b, out, arranged, queries, keys, values,
):
    rows, channels = out.shape
    depth = channels // HEADS

    def put(s, carry):
        row = pl.multiple_of(places[s, 0], UNIT)
        arranged[pl.ds(row, UNIT), :] = arrived[pl.ds(pl.multiple_of(s * UNIT, UNIT), UNIT), :]
        return carry

    lax.fori_loop(0, PEERS * UNITS_PER_PEER, put, 0, unroll=8)
    source = arranged[pl.ds(0, rows), :].astype(f32)
    normed = normalize(source, gain[1:2, :], shift[1:2, :]).astype(bf16)
    joined = (dot(normed, qkv_w[...]) + qkv_b[...]).astype(bf16)
    queries[...] = (joined[:, :channels].astype(f32) * depth ** (-0.5)).astype(bf16)
    turned = jnp.transpose(joined[:, channels : 2 * channels].astype(f32))
    rows_of = lax.broadcasted_iota(jnp.int32, (channels, rows), 0) // depth
    vals = joined[:, 2 * channels :].astype(f32)
    lanes_of = lax.broadcasted_iota(jnp.int32, (rows, channels), 1) // depth
    for h in range(HEADS):
        keys[h] = jnp.where(rows_of == h, turned, 0.0).astype(bf16)
        values[h, :, :channels] = jnp.where(lanes_of == h, vals, 0.0).astype(bf16)
        values[h, :, channels:] = jnp.where(lanes_of == h, 1.0, 0.0).astype(bf16)
    block = 1024

    def row_block(b, carry):
        part = pl.ds(pl.multiple_of(b * block, block), block)
        query = queries[part, :]
        sums = jnp.zeros((block, 2 * channels), f32)
        for h in range(HEADS):
            scores = dot(query, keys[h])
            row_max = jnp.max(scores, axis=-1, keepdims=True)
            weights = jnp.exp(scores - row_max).astype(bf16)
            sums = sums + dot(weights, values[h])
        attended = (sums[:, :channels] / sums[:, channels:]).astype(bf16)
        middle = arranged[part, :].astype(f32) + dot(attended, proj_w[...]) + proj_b[...]
        normed_mid = normalize(middle, gain[2:3, :], shift[2:3, :]).astype(bf16)
        raw = dot(normed_mid, fc1_w[...]) + fc1_b[...]
        hidden = (0.5 * raw * (1.0 + lax.erf(raw * (0.5 ** 0.5)))).astype(bf16)
        out[part, :] = (middle + dot(hidden, fc2_w[...]) + fc2_b[...]).astype(bf16)
        return carry

    lax.fori_loop(0, rows // block, row_block, 0)


def per_device(
    features, positions, neighbors, send_rows, conv_weight, conv_bias, cpe_weight,
    cpe_bias, norm_gain, norm_bias, qkv_weight, qkv_bias, proj_weight, proj_bias,
    fc1_weight, fc1_bias, fc2_weight, fc2_bias,
):
    rows, channels = features.shape
    cores = lax.axis_size("head")
    devs = lax.axis_size("seg") * cores
    width = send_rows.shape[1]
    units = rows // UNIT
    slot_count = PEERS * UNITS_PER_PEER
    dma = pltpu.SemaphoreType.DMA
    unit_places = positions.reshape(units, UNIT)[:, 0]
    limit = 48 * 1024 * 1024

    halo, places, slots = pl.pallas_call(
        functools.partial(halo_kernel, devs, cores),
        out_shape=(
            jax.ShapeDtypeStruct((4 * width, channels), bf16),
            jax.ShapeDtypeStruct((slot_count, 128), jnp.int32),
            jax.ShapeDtypeStruct((1, units), jnp.int32),
        ),
        in_specs=[VM] * 4,
        out_specs=(VM, VM, VM),
        scratch_shapes=[
            pltpu.VMEM((4 * width, channels), bf16),
            pltpu.VMEM((slot_count, 128), jnp.int32),
            pltpu.VMEM((slot_count, 128), jnp.int32),
            dma((4,)), dma((4,)), dma((PEERS,)), dma((PEERS,)),
        ],
        compiler_params=pltpu.CompilerParams(
            collective_id=0, has_side_effects=True, vmem_limit_bytes=limit
        ),
        name="halo",
    )(features, send_rows.T, unit_places[:, None], unit_places[None, :])

    bucket = pl.pallas_call(
        conv_kernel,
        out_shape=jax.ShapeDtypeStruct((slot_count * UNIT, channels), bf16),
        in_specs=[VM, VM, VM, SM] + [VM] * 6,
        out_specs=VM,
        scratch_shapes=[
            pltpu.VMEM(((rows + 4 * width) // 2, 2 * channels), bf16),
            pltpu.VMEM((rows, channels), f32),
            pltpu.VMEM((rows, channels), bf16),
        ],
        compiler_params=pltpu.CompilerParams(vmem_limit_bytes=limit),
        name="conv",
    )(
        features, halo, neighbors, slots, conv_weight, conv_bias[None], cpe_weight,
        cpe_bias[None], norm_gain, norm_bias,
    )

    arrived = pl.pallas_call(
        functools.partial(swap_kernel, devs, cores),
        out_shape=jax.ShapeDtypeStruct(bucket.shape, bf16),
        in_specs=[VM],
        out_specs=VM,
        scratch_shapes=[dma((PEERS,)), dma((PEERS,)), dma],
        compiler_params=pltpu.CompilerParams(
            collective_id=1, has_side_effects=True, vmem_limit_bytes=limit
        ),
        name="swap",
    )(bucket)

    return pl.pallas_call(
        patch_kernel,
        out_shape=jax.ShapeDtypeStruct((rows, channels), bf16),
        in_specs=[SM] + [VM] * 11,
        out_specs=VM,
        scratch_shapes=[
            pltpu.VMEM((rows + UNIT, channels), bf16),
            pltpu.VMEM((rows, channels), bf16),
            pltpu.VMEM((HEADS, channels, rows), bf16),
            pltpu.VMEM((HEADS, rows, 2 * channels), bf16),
        ],
        compiler_params=pltpu.CompilerParams(vmem_limit_bytes=limit),
        name="patch",
    )(
        places, arrived, norm_gain, norm_bias, qkv_weight, qkv_bias[None], proj_weight,
        proj_bias[None], fc1_weight, fc1_bias[None], fc2_weight, fc2_bias[None],
    )


def solution(mesh):
    split = P(("groups", "seg", "head"), None)
    placed = (split, P(("groups", "seg", "head")), split, split) + (P(),) * 14
    return jax.shard_map(
        per_device, mesh=mesh, in_specs=placed, out_specs=split, check_vma=False
    )
```

```python
import functools
import math

import jax
import jax.numpy as jnp
from jax import lax
from jax.experimental import pallas as pl
from jax.experimental.pallas import tpu as pltpu
from jax.sharding import PartitionSpec as P

HEADS = 8
PEERS = 16
BACK = 7
UNITS_PER_PEER = 8
UNIT = 16

norm_epsilon = 1e-05
halo_offsets = (1, 2, -1, -2)
MESH = pl.DeviceIdType.MESH
VM = pl.BlockSpec(memory_space=pltpu.VMEM)
SM = pl.BlockSpec(memory_space=pltpu.SMEM)
f32 = jnp.float32
bf16 = jnp.bfloat16


def normalize(values, norm_scale, norm_shift):
    row_mean = jnp.mean(values, axis=-1, keepdims=True)
    centred = values - row_mean
    spread = jnp.mean(centred * centred, axis=-1, keepdims=True)
    return centred * lax.rsqrt(spread + norm_epsilon) * norm_scale + norm_shift


def dot(a, b):
    return jnp.dot(a, b, preferred_element_type=f32)


def place_of(cores):
    return lax.axis_index("seg") * cores + lax.axis_index("head")


def target(index, cores):
    return {"seg": index // cores, "head": lax.rem(index, cores)}


def greet(me, devs, cores):
    barrier = pltpu.get_barrier_semaphore()
    for label in range(PEERS):
        if label != BACK:
            sender = lax.rem(me - (label - BACK) + devs, devs)
            pl.semaphore_signal(
                barrier, inc=1, device_id=target(sender, cores), device_id_type=MESH
            )
    pl.semaphore_wait(barrier, PEERS - 1)


def halo_kernel(
    devs, cores, feat, picks, ucol, urow, halo, places, slots, outgoing, mine,
    landed, hs, hr, ps, pr,
):
    rows, channels = feat.shape
    width = picks.shape[0]
    me = place_of(cores)
    shift = int(math.log2(rows))
    units = ucol.shape[0]

    def labels(unit_places):
        lab = lax.shift_right_logical(unit_places, jnp.full_like(unit_places, shift)) - me + BACK
        lab = jnp.where(lab < 0, lab + devs, lab)
        return jnp.where(lab >= devs, lab - devs, lab)

    lab_col = labels(ucol[...])
    lab_row = labels(urow[...])
    first = lax.broadcasted_iota(jnp.int32, (units, units), 0)
    second = lax.broadcasted_iota(jnp.int32, (units, units), 1)
    rank = jnp.sum(jnp.where((lab_col == lab_row) & (first < second), 1, 0), axis=0, keepdims=True)
    slot = lab_row * UNITS_PER_PEER + rank
    slots[...] = slot
    slot_ids = lax.broadcasted_iota(jnp.int32, (PEERS * UNITS_PER_PEER, units), 0)
    own = jnp.sum(jnp.where(slot_ids == slot, urow[...] + 1, 0), axis=1, keepdims=True) - 1
    mine[...] = jnp.broadcast_to(own, mine.shape)

    row_ids = lax.broadcasted_iota(jnp.int32, (width, rows), 1)
    for j in range(4):
        table = (picks[:, j : j + 1] == row_ids).astype(f32).astype(bf16)
        outgoing[pl.ds(j * width, width), :] = dot(table, feat[...]).astype(bf16)

    greet(me, devs, cores)

    def halo_copy(j):
        part = pl.ds(j * width, width)
        there = jnp.clip(me + halo_offsets[j], 0, devs - 1)
        return pltpu.make_async_remote_copy(
            src_ref=outgoing.at[part], dst_ref=halo.at[part],
            send_sem=hs.at[j], recv_sem=hr.at[j],
            device_id=target(there, cores), device_id_type=MESH,
        )

    def place_copy(label):
        part = pl.ds(label * UNITS_PER_PEER, UNITS_PER_PEER)
        there = lax.rem(me + (label - BACK) + devs, devs)
        return pltpu.make_async_remote_copy(
            src_ref=mine.at[part], dst_ref=landed.at[part],
            send_sem=ps.at[label], recv_sem=pr.at[label],
            device_id=target(there, cores), device_id_type=MESH,
        )

    def sends(j):
        there = me + halo_offsets[j]
        return (there >= 0) & (there < devs)

    def receives(j):
        source = me - halo_offsets[j]
        return (source >= 0) & (source < devs)

    for j in range(4):
        pl.when(sends(j))(lambda j=j: halo_copy(j).start())
    for label in range(PEERS):
        if label != BACK:
            place_copy(label).start()
    home = pl.ds(BACK * UNITS_PER_PEER, UNITS_PER_PEER)
    landed[home, :] = mine[home, :]
    for j in range(4):
        part = pl.ds(j * width, width)

        @pl.when(jnp.logical_not(receives(j)))
        def _():
            halo[part, :] = jnp.zeros((width, channels), bf16)

    for j in range(4):
        pl.when(sends(j))(lambda j=j: halo_copy(j).wait_send())
        pl.when(receives(j))(lambda j=j: halo_copy(j).wait_recv())
    for label in range(PEERS):
        if label != BACK:
            place_copy(label).wait()
    arrived = landed[...]
    places[...] = jnp.where(arrived >= 0, arrived - me * rows, rows)


def ahead(me, step, devs):
    if devs == PEERS:
        half = devs // 2
        mine = me // half
        across = (1 - mine) * half + lax.rem(me + step, half)
        beside = mine * half + lax.rem(me + step + 1, half)
        return jnp.where(step < half, across, beside)
    return lax.rem(me + jnp.where(step < PEERS // 2, PEERS // 2 - step, PEERS // 2 - 1 - step + devs)
                   + jnp.where(step == PEERS - 1, PEERS // 2 , 0), devs)


def label_of(dest, me, devs):
    return lax.rem(dest - me + BACK + devs, devs)


def swap_kernel(devs, cores, bucket, arrived, ss, rs, ls):
    me = place_of(cores)
    span = bucket.shape[0] // PEERS

    def copy(label):
        part = pl.ds(pl.multiple_of(label * span, span), span)
        there = lax.rem(me + (label - BACK) + devs, devs)
        return pltpu.make_async_remote_copy(
            src_ref=bucket.at[part], dst_ref=arrived.at[part],
            send_sem=ss.at[label], recv_sem=rs.at[label],
            device_id=target(there, cores), device_id_type=MESH,
        )

    greet(me, devs, cores)
    others = [label for label in range(PEERS) if label != BACK]
    for step in range(PEERS - 1):
        copy(label_of(ahead(me, jnp.int32(step), devs), me, devs)).start()
    part = pl.ds(BACK * span, span)
    local = pltpu.make_async_copy(bucket.at[part], arrived.at[part], ls)
    local.start()
    local.wait()
    for label in others:
        copy(label).wait()


def conv_kernel(
    feat, halo, nbr, slots, conv_w, conv_b, cpe_w, cpe_b, gain, shift, bucket,
    table, acc, lifted,
):
    rows, channels = feat.shape
    taps = nbr.shape[1]
    total = rows + halo.shape[0]
    half = total // 2
    table[:, :channels] = feat[pl.ds(0, half), :]
    table[pl.ds(0, rows - half), channels:] = feat[pl.ds(half, rows - half), :]
    table[pl.ds(rows - half, total - rows), channels:] = halo[...]
    centre = taps // 2
    others = [k for k in range(taps) if k != centre]
    block = 512

    def row_block(b, carry):
        part = pl.ds(pl.multiple_of(b * block, block), block)
        lanes = lax.broadcasted_iota(jnp.int32, (block, half), 1)
        total_sum = dot(feat[part, :], conv_w[centre]) + conv_b[...]
        for n in range(0, len(others), 2):
            pair = []
            for k in others[n : n + 2]:
                ids = nbr[part, k : k + 1]
                upper = ids >= half
                local = jnp.where(upper, ids - half, ids)
                hot = (local == lanes).astype(f32).astype(bf16)
                both = dot(hot, table[...])
                pair.append(jnp.where(upper, both[:, channels:], both[:, :channels]).astype(bf16))
            weight = jnp.concatenate([conv_w[k] for k in others[n : n + 2]], axis=0)
            total_sum = total_sum + dot(jnp.concatenate(pair, axis=1), weight)
        encoded = dot(total_sum.astype(bf16), cpe_w[...]) + cpe_b[...]
        own = feat[part, :].astype(f32)
        lifted[part, :] = (own + normalize(encoded, gain[0:1, :], shift[0:1, :])).astype(bf16)
        return carry

    lax.fori_loop(0, rows // block, row_block, 0)
    bucket[...] = jnp.zeros_like(bucket)
    for u in range(rows // UNIT):
        slot = slots[0, u]
        bucket[pl.ds(pl.multiple_of(slot * UNIT, UNIT), UNIT), :] = lifted[pl.ds(u * UNIT, UNIT), :]


def patch_kernel(
    places, arrived, gain, shift, qkv_w, qkv_b, proj_w, proj_b, fc1_w, fc1_b,
    fc2_w, fc2_b, out, arranged, queries, keys, values,
):
    rows, channels = out.shape
    depth = channels // HEADS

    def put(s, carry):
        row = pl.multiple_of(places[s, 0], UNIT)
        arranged[pl.ds(row, UNIT), :] = arrived[pl.ds(pl.multiple_of(s * UNIT, UNIT), UNIT), :]
        return carry

    lax.fori_loop(0, PEERS * UNITS_PER_PEER, put, 0, unroll=8)
    source = arranged[pl.ds(0, rows), :].astype(f32)
    normed = normalize(source, gain[1:2, :], shift[1:2, :]).astype(bf16)
    joined = (dot(normed, qkv_w[...]) + qkv_b[...]).astype(bf16)
    queries[...] = (joined[:, :channels].astype(f32) * depth ** (-0.5)).astype(bf16)
    turned = jnp.transpose(joined[:, channels : 2 * channels].astype(f32))
    rows_of = lax.broadcasted_iota(jnp.int32, (channels, rows), 0) // depth
    vals = joined[:, 2 * channels :].astype(f32)
    lanes_of = lax.broadcasted_iota(jnp.int32, (rows, channels), 1) // depth
    for h in range(HEADS):
        keys[h] = jnp.where(rows_of == h, turned, 0.0).astype(bf16)
        values[h, :, :channels] = jnp.where(lanes_of == h, vals, 0.0).astype(bf16)
        values[h, :, channels:] = jnp.where(lanes_of == h, 1.0, 0.0).astype(bf16)
    block = 1024

    def row_block(b, carry):
        part = pl.ds(pl.multiple_of(b * block, block), block)
        query = queries[part, :]
        sums = jnp.zeros((block, 2 * channels), f32)
        for h in range(HEADS):
            scores = dot(query, keys[h])
            row_max = jnp.max(scores, axis=-1, keepdims=True)
            weights = jnp.exp(scores - row_max).astype(bf16)
            sums = sums + dot(weights, values[h])
        attended = (sums[:, :channels] / sums[:, channels:]).astype(bf16)
        middle = arranged[part, :].astype(f32) + dot(attended, proj_w[...]) + proj_b[...]
        normed_mid = normalize(middle, gain[2:3, :], shift[2:3, :]).astype(bf16)
        raw = dot(normed_mid, fc1_w[...]) + fc1_b[...]
        hidden = (0.5 * raw * (1.0 + lax.erf(raw * (0.5 ** 0.5)))).astype(bf16)
        out[part, :] = (middle + dot(hidden, fc2_w[...]) + fc2_b[...]).astype(bf16)
        return carry

    lax.fori_loop(0, rows // block, row_block, 0)


def per_device(
    features, positions, neighbors, send_rows, conv_weight, conv_bias, cpe_weight,
    cpe_bias, norm_gain, norm_bias, qkv_weight, qkv_bias, proj_weight, proj_bias,
    fc1_weight, fc1_bias, fc2_weight, fc2_bias,
):
    rows, channels = features.shape
    cores = lax.axis_size("head")
    devs = lax.axis_size("seg") * cores
    width = send_rows.shape[1]
    units = rows // UNIT
    slot_count = PEERS * UNITS_PER_PEER
    dma = pltpu.SemaphoreType.DMA
    unit_places = positions.reshape(units, UNIT)[:, 0]
    limit = 48 * 1024 * 1024

    halo, places, slots = pl.pallas_call(
        functools.partial(halo_kernel, devs, cores),
        out_shape=(
            jax.ShapeDtypeStruct((4 * width, channels), bf16),
            jax.ShapeDtypeStruct((slot_count, 128), jnp.int32),
            jax.ShapeDtypeStruct((1, units), jnp.int32),
        ),
        in_specs=[VM] * 4,
        out_specs=(VM, VM, VM),
        scratch_shapes=[
            pltpu.VMEM((4 * width, channels), bf16),
            pltpu.VMEM((slot_count, 128), jnp.int32),
            pltpu.VMEM((slot_count, 128), jnp.int32),
            dma((4,)), dma((4,)), dma((PEERS,)), dma((PEERS,)),
        ],
        compiler_params=pltpu.CompilerParams(
            collective_id=0, has_side_effects=True, vmem_limit_bytes=limit // 6
        ),
        name="halo",
    )(features, send_rows.T, unit_places[:, None], unit_places[None, :])

    bucket = pl.pallas_call(
        conv_kernel,
        out_shape=jax.ShapeDtypeStruct((slot_count * UNIT, channels), bf16),
        in_specs=[VM, VM, VM, SM] + [VM] * 6,
        out_specs=VM,
        scratch_shapes=[
            pltpu.VMEM(((rows + 4 * width) // 2, 2 * channels), bf16),
            pltpu.VMEM((rows, channels), f32),
            pltpu.VMEM((rows, channels), bf16),
        ],
        compiler_params=pltpu.CompilerParams(vmem_limit_bytes=limit),
        name="conv",
    )(
        features, halo, neighbors, slots, conv_weight, conv_bias[None], cpe_weight,
        cpe_bias[None], norm_gain, norm_bias,
    )

    arrived = pl.pallas_call(
        functools.partial(swap_kernel, devs, cores),
        out_shape=jax.ShapeDtypeStruct(bucket.shape, bf16),
        in_specs=[VM],
        out_specs=VM,
        scratch_shapes=[dma((PEERS,)), dma((PEERS,)), dma],
        compiler_params=pltpu.CompilerParams(
            collective_id=1, has_side_effects=True, vmem_limit_bytes=limit // 6
        ),
        name="swap",
    )(bucket)

    return pl.pallas_call(
        patch_kernel,
        out_shape=jax.ShapeDtypeStruct((rows, channels), bf16),
        in_specs=[SM] + [VM] * 11,
        out_specs=VM,
        scratch_shapes=[
            pltpu.VMEM((rows + UNIT, channels), bf16),
            pltpu.VMEM((rows, channels), bf16),
            pltpu.VMEM((HEADS, channels, rows), bf16),
            pltpu.VMEM((HEADS, rows, 2 * channels), bf16),
        ],
        compiler_params=pltpu.CompilerParams(vmem_limit_bytes=limit),
        name="patch",
    )(
        places, arrived, norm_gain, norm_bias, qkv_weight, qkv_bias[None], proj_weight,
        proj_bias[None], fc1_weight, fc1_bias[None], fc2_weight, fc2_bias[None],
    )


def solution(mesh):
    split = P(("groups", "seg", "head"), None)
    placed = (split, P(("groups", "seg", "head")), split, split) + (P(),) * 14
    return jax.shard_map(
        per_device, mesh=mesh, in_specs=placed, out_specs=split, check_vma=False
    )
```
